256 devices in a mesh: batch: 32 (over y_hi, z, core), chan: 8 (over x, y_lo).
Axes of the slice: x: 4, y: 4 (y_hi: 2, y_lo: 2; y = y_hi * 2 + y_lo), z: 8, core: 2. Of those that a mesh axis runs over, the one named last changes fastest.
Arguments:
- token_ids: int32 [4, 128], P(None, 'batch'), may hold values from 0 to 65535
- embed_table: bfloat16 [65536, 8192], P('batch', 'chan'), may hold values from -3 to 3
- norm_gain: float32 [8192], replicated, may hold values from 0.1 to 1.9
- in_weight: bfloat16 [8192, 2, 16384], P('batch', None, 'chan'), may hold values from -0.0625 to 0.0625
- filter_weight: float32 [4, 16384], P(None, 'chan'), may hold values from -3 to 3
- filter_bias: float32 [16384], P('chan'), may hold values from -3 to 3
- select_weight: bfloat16 [16384, 544], P('chan'), may hold values from -0.046875 to 0.046875
- step_gain: float32 [512], replicated, may hold values from 0.1 to 1.9
- step_weight: bfloat16 [512, 16384], P('batch', 'chan'), may hold values from -0.25 to 0.25
- step_bias: float32 [16384], P('chan'), may hold values from -4 to -1
- decay_log: float32 [16, 16384], P(None, 'chan'), may hold values from 0 to 2.77
- skip_gain: float32 [16384], P('chan'), may hold values from 0.5 to 1.5
- out_weight: bfloat16 [16384, 8192], P('chan', 'batch'), may hold values from -0.0234375 to 0.0234375
- filter_state: float32 [128, 3, 16384], P('batch', None, 'chan'), may hold values from -3 to 3
- scan_state: float32 [128, 16, 16384], P('batch', None, 'chan'), may hold values from -3 to 3
Outputs:
- hidden: bfloat16 [4, 128, 8192], P(None, 'batch')
- filter_out: float32 [128, 3, 16384], P('batch', None, 'chan')
- scan_out: float32 [128, 16, 16384], P('batch', None, 'chan')
The draws below stay inside these ranges and needn't reach their ends.
All inputs are finite; a program needn't handle non-finite values.
Results may differ from the reference program's by a relative error of at most 0.0072.
Values may be sent and summed in bfloat16 or wider, within the bound.
No kernel may reach another device: no remote copies, remote signals or barrier semaphores. Data moves between devices by JAX's collectives and lax.ppermute only.
A program may use at most 128 MiB of HBM per device.

```python
import math
import jax
import jax.numpy as jnp
import numpy as np
from jax import lax

D = 8192
E = 16384
N = 16
K = 4
R = 512
VOCAB = 65536
STEPS = 4
REQS = 128


def with_ends(drawn, stream_key, low, top_value):
    place = [jax.random.randint(jax.random.fold_in(stream_key, axis), (), 0, length) for axis, length in enumerate(drawn.shape)]
    widest = drawn.shape.index(max(drawn.shape))
    next_to = place[:widest] + [(place[widest] + 1) % drawn.shape[widest]] + place[widest + 1:]
    return drawn.at[tuple(place)].set(low).at[tuple(next_to)].set(top_value)


def block_scale(stream_key, shape, shards, low, top_value):
    def one(position, blocks):
        heights = jax.random.uniform(jax.random.fold_in(jax.random.fold_in(stream_key, 6), position), (blocks,), jnp.float32, low / len(shards), top_value / len(shards))
        return jnp.repeat(jnp.exp(heights), shape[position] // blocks).reshape((-1,) + (1,) * (len(shape) - position - 1))

    factor_of = one(*shards[0])
    for cut in shards[1:]:
        factor_of = factor_of * one(*cut)
    return factor_of


def rank_bounds(number_of, skew):
    weights = [(1 << 20) // math.isqrt(grade ** skew) + 1 for grade in range(1, number_of + 1)]
    spread = 1 + sum(weights) // (1 << 30)
    return np.cumsum(np.array([max(1, weight // spread) for weight in weights]))


def skewed_ids(rng, extent, count, slope):
    grid = rank_bounds(count, slope)
    ticket = jax.random.randint(jax.random.fold_in(rng, 1), extent, 0, int(grid[count - 1]))
    standing = jnp.searchsorted(jnp.asarray(grid, jnp.int32), ticket, side="right")
    return jax.random.permutation(jax.random.fold_in(rng, 2), count)[standing].astype(jnp.int32)


def scatter_about(rng, shape, deviation, reach, cuts=(), kind=jnp.bfloat16):
    result = deviation * jax.random.normal(rng, shape, jnp.float32)
    if cuts:
        result = result * block_scale(rng, shape, cuts, -0.22, 0.18)
    return jnp.clip(result, -reach, reach).astype(kind)


def setup_inputs(seed: int = 0) -> dict:
    seeds = jax.random.split(jax.random.key(seed), 16)
    return {
        "token_ids": with_ends(skewed_ids(seeds[0], (STEPS, REQS), VOCAB, 2), jax.random.fold_in(seeds[0], 3), 0, VOCAB - 1).astype(jnp.int32),
        "embed_table": scatter_about(seeds[1], (VOCAB, D), 0.5, 3.0, ((0, 32), (1, 8))),
        "norm_gain": jnp.clip(1.0 + 0.18 * jax.random.normal(seeds[2], (D,), jnp.float32), 0.1, 1.9),
        "in_weight": scatter_about(seeds[3], (D, 2, E), D ** -0.5, 0.0625, ((0, 32), (2, 8))),
        "filter_weight": scatter_about(seeds[4], (K, E), K ** -0.5, 3.0, ((1, 8),), jnp.float32),
        "filter_bias": scatter_about(seeds[5], (E,), 0.5, 3.0, ((0, 8),), jnp.float32),
        "select_weight": scatter_about(seeds[6], (E, R + 2 * N), E ** -0.5, 0.046875, ((0, 8),)),
        "step_gain": jnp.clip(1.0 + 0.18 * jax.random.normal(seeds[7], (R,), jnp.float32), 0.1, 1.9),
        "step_weight": scatter_about(seeds[8], (R, E), R ** -0.5, 0.25, ((0, 32), (1, 8))),
        "step_bias": jnp.clip(-4.0 + 3.0 * jax.random.uniform(seeds[9], (E,), jnp.float32) ** block_scale(seeds[9], (E,), ((0, 8),), -0.2, 0.2), -4.0, -1.0),
        "decay_log": jnp.clip(2.77 * jax.random.uniform(seeds[10], (N, E), jnp.float32) ** block_scale(seeds[10], (N, E), ((1, 8),), -0.2, 0.2), 0.0, 2.77),
        "skip_gain": jnp.clip(0.5 + 1.0 * jax.random.uniform(seeds[11], (E,), jnp.float32) ** block_scale(seeds[11], (E,), ((0, 8),), -0.2, 0.2), 0.5, 1.5),
        "out_weight": scatter_about(seeds[12], (E, D), (4 * E) ** -0.5, 0.0234375, ((0, 8), (1, 32))),
        "filter_state": scatter_about(seeds[13], (REQS, K - 1, E), 0.5, 3.0, ((0, 32), (2, 8)), jnp.float32),
        "scan_state": scatter_about(seeds[14], (REQS, N, E), 0.5, 3.0, ((0, 32), (2, 8)), jnp.float32),
    }


def rms_scale(values, gain):
    mean_square = lax.optimization_barrier(jnp.mean(values * values, axis=-1, keepdims=True))
    return values * lax.rsqrt(mean_square + 1e-06) * gain

def reference(token_ids, embed_table, norm_gain, in_weight, filter_weight, filter_bias, select_weight, step_gain, step_weight, step_bias, decay_log, skip_gain, out_weight, filter_state, scan_state):
    decay_rate = -jnp.exp(decay_log)
    filter_now = filter_state
    scan_now = scan_state
    results = []
    for step in range(STEPS):
        embedded = embed_table[token_ids[step]]
        embed_wide = embedded.astype(jnp.float32)
        normed = rms_scale(embed_wide, norm_gain).astype(jnp.bfloat16)
        stream = jnp.dot(normed, in_weight[:, 0, :], preferred_element_type=jnp.float32).astype(jnp.bfloat16)
        gate = jnp.dot(normed, in_weight[:, 1, :], preferred_element_type=jnp.float32).astype(jnp.bfloat16)
        window = jnp.concatenate([filter_now, stream.astype(jnp.float32)[:, None, :]], axis=1)
        convolved = jax.nn.silu(lax.optimization_barrier(jnp.sum(window * filter_weight[None], axis=1)) + filter_bias)
        filter_now = window[:, 1:, :]
        convolved_low = convolved.astype(jnp.bfloat16)
        selected = jnp.dot(convolved_low, select_weight, preferred_element_type=jnp.float32)
        rank = selected[:, :R]
        bvec = selected[:, R:R + N]
        cvec = selected[:, R + N:]
        rank_normed = rms_scale(rank, step_gain).astype(jnp.bfloat16)
        delta = jax.nn.softplus(jnp.dot(rank_normed, step_weight, preferred_element_type=jnp.float32) + step_bias)
        factor = jnp.exp(delta[:, None, :] * decay_rate[None])
        scan_now = factor * scan_now + (delta * convolved)[:, None, :] * bvec[:, :, None]
        readout = lax.optimization_barrier(jnp.sum(scan_now * cvec[:, :, None], axis=1)) + skip_gain * convolved
        gated = (readout * jax.nn.silu(gate.astype(jnp.float32))).astype(jnp.bfloat16)
        mixed = jnp.dot(gated, out_weight, preferred_element_type=jnp.float32).astype(jnp.bfloat16)
        results.append((embed_wide + mixed.astype(jnp.float32)).astype(jnp.bfloat16))
    return (jnp.stack(results), filter_now, scan_now)
```

```python
import jax
import jax.numpy as jnp
from jax import lax
from jax.sharding import Mesh, PartitionSpec as P

BATCH = ("h", "z", "k")
CHAN = ("x", "l")
SIZES = {"h": 2, "z": 8, "k": 2, "x": 4, "l": 2}
AXES = BATCH + CHAN
F32 = jnp.float32
BF16 = jnp.bfloat16


def count(axes):
    total = 1
    for axis in axes:
        total *= SIZES[axis]
    return total


def gather_copies(block, axes):
    copies = jnp.broadcast_to(block[None], (count(axes),) + block.shape)
    return lax.all_to_all(copies, axes, 0, 0, tiled=True)


def swap(block, axis):
    return lax.ppermute(block, axis, [(0, 1), (1, 0)])


def feature_route():
    pairs = []
    for b in range(32):
        for c in range(8):
            pairs.append((b * 8 + c, (4 * c + b // 8) * 8 + b % 8))
    return pairs


def ring_gather(block, axis):
    n = SIZES[axis]
    up = [(i, (i + 1) % n) for i in range(n)]
    down = [(i, (i - 1) % n) for i in range(n)]
    found = {0: block}
    a = b = block
    for step in range(1, n // 2 + 1):
        a = lax.ppermute(a, axis, up)
        found[-step % n] = a
        if step < n // 2:
            b = lax.ppermute(b, axis, down)
            found[step] = b
    return [found[i] for i in range(n)]


def local(
    token_ids,
    embed_table,
    norm_gain,
    in_weight,
    filter_weight,
    filter_bias,
    select_weight,
    step_gain,
    step_weight,
    step_bias,
    decay_log,
    skip_gain,
    out_weight,
    filter_state,
    scan_state,
):
    steps, reqs = token_ids.shape
    vocab_rows, width = embed_table.shape
    feats, _, channels = in_weight.shape
    half = channels // 2
    rank_size = step_gain.shape[0]
    state_size = decay_log.shape[0]
    rows = steps * reqs
    nb, nc = count(BATCH), count(CHAN)
    tokens = nb * rows
    core = lax.axis_index("k")
    me = lax.axis_index(BATCH)
    features = norm_gain.shape[0]

    step_full = lax.all_gather(step_weight, BATCH, axis=0, tiled=True)
    halves = in_weight.reshape(feats, 2, 2, half)
    w_mine = lax.dynamic_index_in_dim(halves, core, axis=2, keepdims=False)
    w_other = swap(lax.dynamic_index_in_dim(halves, 1 - core, axis=2, keepdims=False), "k")

    ids = gather_copies(token_ids.reshape(rows), BATCH).reshape(tokens)
    vocab_index = me * vocab_rows + lax.broadcasted_iota(jnp.int32, (vocab_rows, tokens), 0)
    hot = (vocab_index == ids[None, :]).astype(BF16)
    picked = lax.dot_general(
        embed_table, hot, (((0,), (0,)), ((), ())), preferred_element_type=F32
    ).astype(BF16)
    pieces = lax.all_to_all(picked.reshape(nb, width // nb, tokens), BATCH, 0, 0, tiled=True)
    piece = jnp.sum(pieces.astype(F32), axis=0).astype(BF16)
    piece = lax.ppermute(piece, AXES, feature_route())
    chip_feats = gather_copies(piece, ("k",) + CHAN).reshape(2, feats, tokens)

    wide = chip_feats.astype(F32)
    square = jnp.sum(wide * wide, axis=(0, 1))
    gains = lax.dynamic_slice_in_dim(norm_gain, (me - core) * feats, 2 * feats).reshape(2, feats)
    scaled = (wide * gains[:, :, None]).astype(BF16)
    x_mine = lax.dynamic_index_in_dim(scaled, core, keepdims=False)
    x_other = lax.dynamic_index_in_dim(scaled, 1 - core, keepdims=False)
    own_feats = lax.dynamic_index_in_dim(chip_feats, core, keepdims=False)

    def project(which):
        dims = (((0,), (0,)), ((), ()))
        return lax.dot_general(
            x_mine, w_mine[:, which], dims, preferred_element_type=F32
        ) + lax.dot_general(x_other, w_other[:, which], dims, preferred_element_type=F32)

    def exchange(part):
        sent = part.astype(BF16).reshape(nb, rows, part.shape[1])
        got = lax.all_to_all(sent, BATCH, 0, 0, tiled=True)
        return got.reshape(nb // 2, 2, rows, part.shape[1]).astype(F32)

    square = square[:, None]
    high = square.astype(BF16)
    low = (square - high.astype(F32)).astype(BF16)
    lane = lax.broadcasted_iota(jnp.int32, (1, 128), 1)
    tail = jnp.where(lane == 0, high, jnp.where(lane == 1, low, 0.0)).astype(F32)
    got = exchange(jnp.concatenate([project(0), tail], axis=1))
    summed = jnp.sum(got, axis=0)
    total = jnp.sum(summed[0, :, half : half + 2], axis=1, keepdims=True)
    scale = lax.rsqrt(total / features + 1e-06)

    def finish(two):
        return (jnp.concatenate([two[0], two[1]], axis=1) * scale).astype(BF16).astype(F32)

    stream = finish(summed[:, :, :half])
    gate_part = project(1)
    gate = finish(jnp.sum(exchange(gate_part), axis=0))

    stream = stream.reshape(steps, reqs, channels)
    window = jnp.concatenate([filter_state.transpose(1, 0, 2), stream], axis=0)
    taps = filter_weight.shape[0]
    mixed_in = sum(window[i : i + steps] * filter_weight[i] for i in range(taps))
    convolved = jax.nn.silu(mixed_in + filter_bias)
    filter_out = window[steps:].transpose(1, 0, 2)
    conv_rows = convolved.reshape(rows, channels)
    part = jnp.dot(conv_rows.astype(BF16), select_weight, preferred_element_type=F32)
    selected = jnp.sum(gather_copies(part, CHAN), axis=0)
    rank = selected[:, :rank_size]
    bvec = selected[:, rank_size : rank_size + state_size].reshape(steps, reqs, state_size)
    cvec = selected[:, rank_size + state_size :].reshape(steps, reqs, state_size)
    mean_square = jnp.mean(rank * rank, axis=-1, keepdims=True)
    rank_normed = (rank * lax.rsqrt(mean_square + 1e-06) * step_gain).astype(BF16)
    delta = jax.nn.softplus(
        jnp.dot(rank_normed, step_full, preferred_element_type=F32) + step_bias
    ).reshape(steps, reqs, channels)

    decay_rate = -jnp.exp(decay_log)
    scan_now = scan_state
    readouts = []
    for t in range(steps):
        factor = jnp.exp(delta[t][:, None, :] * decay_rate[None])
        scan_now = factor * scan_now + (delta[t] * convolved[t])[:, None, :] * bvec[t][:, :, None]
        readouts.append(jnp.sum(scan_now * cvec[t][:, :, None], axis=1) + skip_gain * convolved[t])
    readout = jnp.stack(readouts).reshape(rows, channels)
    gated = (readout * jax.nn.silu(gate)).astype(BF16)

    both = jnp.stack([gated, swap(gated, "h")])
    ring = jnp.stack(ring_gather(both, "z"))
    every = jnp.stack([ring, swap(ring, "k")])
    part_out = jnp.dot(
        every.reshape(tokens, channels), out_weight, preferred_element_type=F32
    ).astype(BF16)
    per = rows // nc
    sent = part_out.reshape(nb, nc, per, feats).transpose(1, 0, 2, 3)
    got = lax.all_to_all(sent, CHAN, 0, 0, tiled=True)
    mixed = jnp.sum(got.astype(F32), axis=0).astype(BF16)

    z, h = lax.axis_index("z"), lax.axis_index("h")
    dest = lax.broadcasted_iota(jnp.int32, (nb, 1), 0)
    source = lax.broadcasted_iota(jnp.int32, (1, nb), 1)
    s_k, s_z, s_h = source // 16, (source // 2) % 8, source % 2
    place = ((s_h + h) % 2) * 16 + ((s_z + z) % 8) * 2 + (s_k + core) % 2
    order = (dest == place).astype(BF16)
    mixed = jnp.dot(order, mixed.reshape(nb, per * feats), preferred_element_type=F32)
    mixed = mixed.reshape(nb * per, feats)
    column = lax.axis_index(CHAN)
    row = lax.broadcasted_iota(jnp.int32, (nb * per, 1), 0)
    token = lax.broadcasted_iota(jnp.int32, (1, tokens), 1)
    pick = (token == (row // per) * rows + column * per + row % per).astype(BF16)
    embedded = lax.dot_general(
        pick, own_feats, (((1,), (1,)), ((), ())), preferred_element_type=F32
    )
    hidden = (embedded + mixed).astype(BF16).reshape(nb, per, feats)
    home = lax.all_to_all(hidden, BATCH, 0, 0, tiled=True)
    home = home.transpose(1, 0, 2).reshape(per, nb * feats)
    hidden = gather_copies(home, CHAN).reshape(steps, reqs, features)
    return (hidden, filter_out, scan_now)


def solution(mesh):
    fine = Mesh(mesh.devices.reshape([SIZES[axis] for axis in AXES]), AXES)
    return jax.shard_map(
        local,
        mesh=fine,
        in_specs=(
            P(None, BATCH),
            P(BATCH, CHAN),
            P(),
            P(BATCH, None, CHAN),
            P(None, CHAN),
            P(CHAN),
            P(CHAN, None),
            P(),
            P(BATCH, CHAN),
            P(CHAN),
            P(None, CHAN),
            P(CHAN),
            P(CHAN, BATCH),
            P(BATCH, None, CHAN),
            P(BATCH, None, CHAN),
        ),
        out_specs=(P(None, BATCH, None), P(BATCH, None, CHAN), P(BATCH, None, CHAN)),
        check_vma=False,
    )
```

```python
import jax
import jax.numpy as jnp
from jax import lax
from jax.sharding import Mesh, PartitionSpec as P

BATCH = ("h", "z", "k")
CHAN = ("x", "l")
SIZES = {"h": 2, "z": 8, "k": 2, "x": 4, "l": 2}
AXES = BATCH + CHAN
F32 = jnp.float32
BF16 = jnp.bfloat16


def count(axes):
    total = 1
    for axis in axes:
        total *= SIZES[axis]
    return total


def gather_copies(block, axes):
    copies = jnp.broadcast_to(block[None], (count(axes),) + block.shape)
    return lax.all_to_all(copies, axes, 0, 0, tiled=True)


def swap(block, axis):
    return lax.ppermute(block, axis, [(0, 1), (1, 0)])


def shift(block, axis, distance):
    n = SIZES[axis]
    return lax.ppermute(block, axis, [(i, (i + distance) % n) for i in range(n)])


def take(block, index):
    return lax.dynamic_index_in_dim(block, index, keepdims=False)


def add(a, b):
    return (a.astype(F32) + b.astype(F32)).astype(BF16)


def ring_sums(parts, axis):
    n = SIZES[axis]
    here = lax.axis_index(axis)
    up = [None] * len(parts)
    down = [None] * len(parts)
    for away in range(n // 2, 0, -1):
        for i, part in enumerate(parts):
            term = take(part, (here + away) % n)
            up[i] = shift(term if up[i] is None else add(term, up[i]), axis, 1)
            if away < n // 2:
                term = take(part, (here - away) % n)
                down[i] = shift(term if down[i] is None else add(term, down[i]), axis, -1)
    return [
        (take(part, here).astype(F32) + u.astype(F32) + d.astype(F32)).astype(BF16)
        for part, u, d in zip(parts, up, down)
    ]


def local(
    token_ids,
    embed_table,
    norm_gain,
    in_weight,
    filter_weight,
    filter_bias,
    select_weight,
    step_gain,
    step_weight,
    step_bias,
    decay_log,
    skip_gain,
    out_weight,
    filter_state,
    scan_state,
):
    steps, reqs = token_ids.shape
    vocab_rows, width = embed_table.shape
    feats, _, channels = in_weight.shape
    half = channels // 2
    rank_size = step_gain.shape[0]
    state_size = decay_log.shape[0]
    rows = steps * reqs
    nb, nc = count(BATCH), count(CHAN)
    tokens = nb * rows
    core = lax.axis_index("k")
    me = lax.axis_index(BATCH)
    features = norm_gain.shape[0]

    step_full = lax.all_gather(step_weight, BATCH, axis=0, tiled=True)
    in_flat = in_weight.reshape(feats, 2 * channels)

    ids = gather_copies(token_ids.reshape(rows), BATCH).reshape(nb // 2, 2, rows)
    ids = ids.transpose(1, 0, 2).reshape(tokens)
    ids, in_flat = lax.optimization_barrier((ids, in_flat))
    vocab_index = me * vocab_rows + lax.broadcasted_iota(jnp.int32, (tokens, vocab_rows), 1)
    hot = (vocab_index == ids[:, None]).astype(BF16)
    picked = jnp.dot(hot, embed_table, preferred_element_type=F32).astype(BF16)
    picked = picked.reshape(2, nb // 2, rows, width)
    picked = add(take(picked, core), swap(take(picked, 1 - core), "k"))
    picked = lax.all_to_all(picked, ("h", "z"), 0, 0, tiled=True)
    own = jnp.sum(picked.astype(F32), axis=0).astype(BF16)
    embedded = gather_copies(own, CHAN).transpose(1, 0, 2).reshape(rows, features)
    embed_wide = embedded.astype(F32)
    mean_square = jnp.mean(embed_wide * embed_wide, axis=-1, keepdims=True)
    normed = (embed_wide * lax.rsqrt(mean_square + 1e-06) * norm_gain).astype(BF16)
    spread = normed.reshape(rows, nb, feats).transpose(1, 0, 2)
    x = lax.all_to_all(spread, BATCH, 0, 0, tiled=True).reshape(tokens, feats)
    x, step_full = lax.optimization_barrier((x, step_full))

    side = lax.axis_index("h")

    def project(which, part_of):
        w = lax.dynamic_slice_in_dim(in_flat, which * channels + part_of * half, half, axis=1)
        part = jnp.dot(x, w, preferred_element_type=F32).astype(BF16)
        return part.reshape(2, 8, 2 * rows, half)

    theirs = [swap(project(which, 1 - core), "k") for which in range(2)]
    parts = [add(project(which, core), theirs[which]) for which in range(2)]
    sums = ring_sums([part.transpose(1, 0, 2, 3) for part in parts], "z")
    sums = [add(take(one, side), swap(take(one, 1 - side), "h")) for one in sums]
    both = jnp.stack(sums).reshape(2, 2, rows, half)
    mine = lax.dynamic_index_in_dim(both, core, axis=1, keepdims=False)
    other = swap(lax.dynamic_index_in_dim(both, 1 - core, axis=1, keepdims=False), "k")
    first = jnp.where(core == 0, mine, other)
    last = jnp.where(core == 0, other, mine)
    stream = jnp.concatenate([first[0], last[0]], axis=1).astype(F32)
    gate = jnp.concatenate([first[1], last[1]], axis=1).astype(F32)

    stream = stream.reshape(steps, reqs, channels)
    window = jnp.concatenate([filter_state.transpose(1, 0, 2), stream], axis=0)
    taps = filter_weight.shape[0]
    mixed_in = sum(window[i : i + steps] * filter_weight[i] for i in range(taps))
    convolved = jax.nn.silu(mixed_in + filter_bias)
    filter_out = window[steps:].transpose(1, 0, 2)
    conv_rows = convolved.reshape(rows, channels)
    part = jnp.dot(conv_rows.astype(BF16), select_weight, preferred_element_type=F32)
    selected = jnp.sum(gather_copies(part, CHAN), axis=0)
    rank = selected[:, :rank_size]
    bvec = selected[:, rank_size : rank_size + state_size].reshape(steps, reqs, state_size)
    cvec = selected[:, rank_size + state_size :].reshape(steps, reqs, state_size)
    mean_square = jnp.mean(rank * rank, axis=-1, keepdims=True)
    rank_normed = (rank * lax.rsqrt(mean_square + 1e-06) * step_gain).astype(BF16)
    delta = jax.nn.softplus(
        jnp.dot(rank_normed, step_full, preferred_element_type=F32) + step_bias
    ).reshape(steps, reqs, channels)

    decay_rate = -jnp.exp(decay_log)
    scan_now = scan_state
    readouts = []
    for t in range(steps):
        factor = jnp.exp(delta[t][:, None, :] * decay_rate[None])
        scan_now = factor * scan_now + (delta[t] * convolved[t])[:, None, :] * bvec[t][:, :, None]
        readouts.append(jnp.sum(scan_now * cvec[t][:, :, None], axis=1) + skip_gain * convolved[t])
    readout = jnp.stack(readouts).reshape(rows, channels)
    gated = (readout * jax.nn.silu(gate)).astype(BF16)

    every = lax.all_gather(gated, "z")
    every = jnp.stack([every, swap(every, "h")])
    every = jnp.stack([every, swap(every, "k")])
    part_out = jnp.dot(
        every.reshape(tokens, channels), out_weight, preferred_element_type=F32
    ).astype(BF16)
    per = rows // nc
    sent = part_out.reshape(nb, nc, per, feats).transpose(1, 0, 2, 3)
    got = lax.all_to_all(sent, CHAN, 0, 0, tiled=True)
    mixed = jnp.sum(got.astype(F32), axis=0).astype(BF16)

    dest = lax.broadcasted_iota(jnp.int32, (nb, 1), 0)
    source = lax.broadcasted_iota(jnp.int32, (1, nb), 1)
    s_k, s_h, s_z = source // 16, (source // 8) % 2, source % 8
    place = ((s_h + side) % 2) * 16 + s_z * 2 + (s_k + core) % 2
    order = (dest == place).astype(BF16)
    mixed = jnp.dot(order, mixed.reshape(nb, per * feats), preferred_element_type=F32)
    mixed = mixed.astype(BF16).reshape(nb, 1, per, feats)
    copies = jnp.broadcast_to(mixed, (nb, nc, per, feats)).reshape(nb * nc, per, feats)
    home = lax.all_to_all(copies, AXES, 0, 0, tiled=True).reshape(nb, nc * per, feats)
    home = home.transpose(1, 0, 2).reshape(rows, features)
    hidden = (embed_wide + home.astype(F32)).astype(BF16).reshape(steps, reqs, features)
    return (hidden, filter_out, scan_now)


def solution(mesh):
    fine = Mesh(mesh.devices.reshape([SIZES[axis] for axis in AXES]), AXES)
    return jax.shard_map(
        local,
        mesh=fine,
        in_specs=(
            P(None, BATCH),
            P(BATCH, CHAN),
            P(),
            P(BATCH, None, CHAN),
            P(None, CHAN),
            P(CHAN),
            P(CHAN, None),
            P(),
            P(BATCH, CHAN),
            P(CHAN),
            P(None, CHAN),
            P(CHAN),
            P(CHAN, BATCH),
            P(BATCH, None, CHAN),
            P(BATCH, None, CHAN),
        ),
        out_specs=(P(None, BATCH, None), P(BATCH, None, CHAN), P(BATCH, None, CHAN)),
        check_vma=False,
    )
```

```python
import jax
import jax.numpy as jnp
from jax import lax
from jax.sharding import Mesh, PartitionSpec as P

BATCH = ("h", "z", "k")
CHAN = ("x", "l")
SIZES = {"h": 2, "z": 8, "k": 2, "x": 4, "l": 2}
AXES = BATCH + CHAN
F32 = jnp.float32
BF16 = jnp.bfloat16


def count(axes):
    total = 1
    for axis in axes:
        total *= SIZES[axis]
    return total


def gather_copies(block, axes):
    copies = jnp.broadcast_to(block[None], (count(axes),) + block.shape)
    return lax.all_to_all(copies, axes, 0, 0, tiled=True)


def swap(block, axis):
    return lax.ppermute(block, axis, [(0, 1), (1, 0)])


def shift(block, axis, distance):
    n = SIZES[axis]
    return lax.ppermute(block, axis, [(i, (i + distance) % n) for i in range(n)])


def in_order(mine, other, index):
    first = jnp.where(index == 0, mine, other)
    return jnp.concatenate([first, jnp.where(index == 0, other, mine)])


def take(block, index):
    return lax.dynamic_index_in_dim(block, index, keepdims=False)


def add(a, b):
    return (a.astype(F32) + b.astype(F32)).astype(BF16)


def ring_sums(parts, axis):
    n = SIZES[axis]
    here = lax.axis_index(axis)
    up = [None] * len(parts)
    down = [None] * len(parts)
    for away in range(n // 2, 0, -1):
        for i, part in enumerate(parts):
            term = take(part, (here + away) % n)
            up[i] = shift(term if up[i] is None else add(term, up[i]), axis, 1)
            if away < n // 2:
                term = take(part, (here - away) % n)
                down[i] = shift(term if down[i] is None else add(term, down[i]), axis, -1)
    return [
        (take(part, here).astype(F32) + u.astype(F32) + d.astype(F32)).astype(BF16)
        for part, u, d in zip(parts, up, down)
    ]


def local(
    token_ids,
    embed_table,
    norm_gain,
    in_weight,
    filter_weight,
    filter_bias,
    select_weight,
    step_gain,
    step_weight,
    step_bias,
    decay_log,
    skip_gain,
    out_weight,
    filter_state,
    scan_state,
):
    steps, reqs = token_ids.shape
    vocab_rows, width = embed_table.shape
    feats, _, channels = in_weight.shape
    rank_size = step_gain.shape[0]
    state_size = decay_log.shape[0]
    rows = steps * reqs
    nb, nc = count(BATCH), count(CHAN)
    tokens = nb * rows
    core = lax.axis_index("k")
    me = lax.axis_index(BATCH)
    features = norm_gain.shape[0]

    side = lax.axis_index("h")
    step_rows = in_order(step_weight, swap(step_weight, "k"), core)
    step_rows = in_order(step_rows, swap(step_rows, "h"), side)
    step_full = lax.all_gather(step_rows, "z", axis=0, tiled=True)
    in_flat = in_weight.reshape(feats, 2 * channels)

    ids = gather_copies(token_ids.reshape(rows), BATCH).reshape(nb // 2, 2, rows)
    ids = ids.transpose(1, 0, 2).reshape(tokens)
    ids, in_flat = lax.optimization_barrier((ids, in_flat))
    in_other = swap(in_flat, "k")
    out_pair = jnp.stack([out_weight, swap(out_weight, "k")])
    out_far = swap(out_pair, "h")
    vocab_index = me * vocab_rows + lax.broadcasted_iota(jnp.int32, (tokens, vocab_rows), 1)
    hot = (vocab_index == ids[:, None]).astype(BF16)
    picked = jnp.dot(hot, embed_table, preferred_element_type=F32).astype(BF16)
    picked = picked.reshape(2, nb // 2, rows, width)
    picked = add(take(picked, core), swap(take(picked, 1 - core), "k"))
    picked = lax.all_to_all(picked, ("h", "z"), 0, 0, tiled=True)
    own = jnp.sum(picked.astype(F32), axis=0).astype(BF16)
    embedded = gather_copies(own, CHAN).transpose(1, 0, 2).reshape(rows, features)
    embed_wide = embedded.astype(F32)
    mean_square = jnp.mean(embed_wide * embed_wide, axis=-1, keepdims=True)
    normed = (embed_wide * lax.rsqrt(mean_square + 1e-06) * norm_gain).astype(BF16)
    spread = normed.reshape(rows, nb // 2, 2 * feats).transpose(1, 0, 2)
    x = lax.all_to_all(spread, ("h", "z"), 0, 0, tiled=True).reshape(tokens // 2, 2 * feats)
    x_mine = lax.dynamic_slice_in_dim(x, core * feats, feats, axis=1)
    x_other = lax.dynamic_slice_in_dim(x, (1 - core) * feats, feats, axis=1)


    def project(which):
        cols = slice(which * channels, (which + 1) * channels)
        part = jnp.dot(x_mine, in_flat[:, cols], preferred_element_type=F32)
        part += jnp.dot(x_other, in_other[:, cols], preferred_element_type=F32)
        return part.astype(BF16).reshape(2, 8, rows, channels).transpose(1, 0, 2, 3)

    first, step_full = lax.optimization_barrier((project(0), step_full))
    sums = ring_sums([first, project(1)], "z")
    stream, gate = [
        add(take(one, side), swap(take(one, 1 - side), "h")).astype(F32) for one in sums
    ]

    stream = stream.reshape(steps, reqs, channels)
    window = jnp.concatenate([filter_state.transpose(1, 0, 2), stream], axis=0)
    taps = filter_weight.shape[0]
    mixed_in = sum(window[i : i + steps] * filter_weight[i] for i in range(taps))
    convolved = jax.nn.silu(mixed_in + filter_bias)
    filter_out = window[steps:].transpose(1, 0, 2)
    conv_rows = convolved.reshape(rows, channels)
    part = jnp.dot(conv_rows.astype(BF16), select_weight, preferred_element_type=F32)
    selected = jnp.sum(gather_copies(part, CHAN), axis=0)
    rank = selected[:, :rank_size]
    bvec = selected[:, rank_size : rank_size + state_size].reshape(steps, reqs, state_size)
    cvec = selected[:, rank_size + state_size :].reshape(steps, reqs, state_size)
    mean_square = jnp.mean(rank * rank, axis=-1, keepdims=True)
    rank_normed = (rank * lax.rsqrt(mean_square + 1e-06) * step_gain).astype(BF16)
    rank_normed = rank_normed.reshape(rows, 2, 8, rank_size // 16)
    rank_normed = rank_normed.transpose(0, 2, 1, 3).reshape(rows, rank_size)
    delta = jax.nn.softplus(
        jnp.dot(rank_normed, step_full, preferred_element_type=F32) + step_bias
    ).reshape(steps, reqs, channels)

    decay_rate = -jnp.exp(decay_log)
    scan_now = scan_state
    readouts = []
    for t in range(steps):
        factor = jnp.exp(delta[t][:, None, :] * decay_rate[None])
        scan_now = factor * scan_now + (delta[t] * convolved[t])[:, None, :] * bvec[t][:, :, None]
        readouts.append(jnp.sum(scan_now * cvec[t][:, :, None], axis=1) + skip_gain * convolved[t])
    readout = jnp.stack(readouts).reshape(rows, channels)
    gated = (readout * jax.nn.silu(gate)).astype(BF16)

    every = lax.all_gather(gated, "z").reshape(8 * rows, channels)
    blocks = [out_pair[0], out_pair[1], out_far[0], out_far[1]]
    part_out = [jnp.dot(every, w, preferred_element_type=F32).astype(BF16) for w in blocks]
    per = rows // nc
    sent = jnp.concatenate(part_out, axis=1).reshape(8, nc, per, 4 * feats).transpose(1, 0, 2, 3)
    got = lax.all_to_all(sent, CHAN, 0, 0, tiled=True)
    mixed = jnp.sum(got.astype(F32), axis=0).astype(BF16).reshape(8, per, 2, 2, feats)
    mixed = jnp.where(core == 0, mixed, mixed[:, :, :, ::-1])
    mixed = jnp.where(side == 0, mixed, mixed[:, :, ::-1]).reshape(8, 1, per, 4 * feats)

    copies = jnp.broadcast_to(mixed, (8, nc, per, 4 * feats)).reshape(8 * nc, per, 4 * feats)
    home = lax.all_to_all(copies, ("z",) + CHAN, 0, 0, tiled=True)
    home = home.reshape(8, rows, 2, 2 * feats).transpose(1, 2, 0, 3).reshape(rows, features)
    hidden = (embed_wide + home.astype(F32)).astype(BF16).reshape(steps, reqs, features)
    return (hidden, filter_out, scan_now)


def solution(mesh):
    fine = Mesh(mesh.devices.reshape([SIZES[axis] for axis in AXES]), AXES)
    return jax.shard_map(
        local,
        mesh=fine,
        in_specs=(
            P(None, BATCH),
            P(BATCH, CHAN),
            P(),
            P(BATCH, None, CHAN),
            P(None, CHAN),
            P(CHAN),
            P(CHAN, None),
            P(),
            P(BATCH, CHAN),
            P(CHAN),
            P(None, CHAN),
            P(CHAN),
            P(CHAN, BATCH),
            P(BATCH, None, CHAN),
            P(BATCH, None, CHAN),
        ),
        out_specs=(P(None, BATCH, None), P(BATCH, None, CHAN), P(BATCH, None, CHAN)),
        check_vma=False,
    )
```

```python
import jax
import jax.numpy as jnp
from jax import lax
from jax.experimental import pallas as pl
from jax.experimental.pallas import tpu as pltpu
from jax.sharding import Mesh, PartitionSpec as P

BATCH = ("h", "z", "k")
CHAN = ("x", "l")
SIZES = {"h": 2, "z": 8, "k": 2, "x": 4, "l": 2}
AXES = BATCH + CHAN
F32 = jnp.float32
BF16 = jnp.bfloat16


def count(axes):
    total = 1
    for axis in axes:
        total *= SIZES[axis]
    return total


def gather_copies(block, axes):
    copies = jnp.broadcast_to(block[None], (count(axes),) + block.shape)
    return lax.all_to_all(copies, axes, 0, 0, tiled=True)


def swap(block, axis):
    return lax.ppermute(block, axis, [(0, 1), (1, 0)])


def shift(block, axis, distance):
    n = SIZES[axis]
    return lax.ppermute(block, axis, [(i, (i + distance) % n) for i in range(n)])


def in_order(mine, other, index, axis):
    first = jnp.where(index == 0, mine, other)
    return jnp.concatenate([first, jnp.where(index == 0, other, mine)], axis=axis)


def take(block, index):
    return lax.dynamic_index_in_dim(block, index, keepdims=False)


def add(a, b):
    return (a.astype(F32) + b.astype(F32)).astype(BF16)


def ring_sums(parts, axis):
    n = SIZES[axis]
    here = lax.axis_index(axis)
    up = [None] * len(parts)
    down = [None] * len(parts)
    for away in range(n // 2, 0, -1):
        if up[0] is not None:
            up[0], down[0] = lax.optimization_barrier((up[0], down[0]))
        for i, part in enumerate(parts):
            term = take(part, (here + away) % n)
            up[i] = shift(term if up[i] is None else add(term, up[i]), axis, 1)
            if away < n // 2:
                term = take(part, (here - away) % n)
                down[i] = shift(term if down[i] is None else add(term, down[i]), axis, -1)
    return [
        (take(part, here).astype(F32) + u.astype(F32) + d.astype(F32)).astype(BF16)
        for part, u, d in zip(parts, up, down)
    ]


def convolve_kernel(mine_ref, got_ref, past_ref, taps_ref, bias_ref, select_ref, conv_ref, past_out_ref, part_ref):
    kept, reqs, _ = past_ref.shape
    rows = mine_ref.shape[0]
    steps = rows // reqs
    stream = (mine_ref[...].astype(F32) + got_ref[...].astype(F32)).astype(BF16).astype(F32)
    window = [past_ref[i] for i in range(kept)]
    window += [stream[i * reqs : (i + 1) * reqs] for i in range(steps)]
    for i in range(kept):
        past_out_ref[i] = window[steps + i]
    found = []
    for t in range(steps):
        total = window[t] * taps_ref[0:1, :]
        for i in range(1, kept + 1):
            total += window[t + i] * taps_ref[i : i + 1, :]
        total += bias_ref[...]
        found.append(total * jax.nn.sigmoid(total))
    convolved = jnp.concatenate(found, axis=0)
    conv_ref[...] = convolved
    low = convolved.astype(BF16)
    rank_size = part_ref.shape[2] - 128
    turned = (((1,), (1,)), ((), ()))
    rank = lax.dot_general(low, select_ref[:rank_size, :], turned, preferred_element_type=F32)
    rest = lax.dot_general(low, select_ref[rank_size:, :], turned, preferred_element_type=F32)
    rest = jnp.concatenate([rest, jnp.zeros((rows, 128 - rest.shape[1]), F32)], axis=1)
    for i in range(part_ref.shape[0]):
        part_ref[i, :, :rank_size] = rank
        part_ref[i, :, rank_size:] = rest


def convolve(mine, got, past, taps, bias, select, rank_size, copies):
    rows, channels = mine.shape
    width = rank_size + 128
    return pl.pallas_call(
        convolve_kernel,
        out_shape=(
            jax.ShapeDtypeStruct((rows, channels), F32),
            jax.ShapeDtypeStruct(past.shape, F32),
            jax.ShapeDtypeStruct((copies, rows, width), F32),
        ),
        compiler_params=pltpu.CompilerParams(vmem_limit_bytes=24 * 1024 * 1024),
        cost_estimate=pl.CostEstimate(
            flops=2 * rows * channels * width,
            bytes_accessed=2 * channels * width,
            transcendentals=rows * channels,
        ),
        name="convolve",
    )(mine, got, past, taps, bias[None], select)


def scan_kernel(
    got_ref, gain_ref, step_ref, bias_ref, decay_ref, skip_ref, conv_ref, gate_ref, gate_got_ref, state_ref,
    gated_ref, state_out_ref, weight_ref,
):
    reqs, states, _ = state_ref.shape
    rows = conv_ref.shape[0]
    rank_size = gain_ref.shape[1]
    turns, sides, tall, _ = step_ref.shape
    for z in range(turns):
        for h in range(sides):
            first = (h * turns + z) * tall
            weight_ref[first : first + tall, :] = step_ref[z, h]
    selected = got_ref[0]
    for i in range(1, got_ref.shape[0]):
        selected += got_ref[i]
    rank = selected[:, :rank_size]
    mean_square = jnp.mean(rank * rank, axis=-1, keepdims=True)
    normed = (rank * lax.rsqrt(mean_square + 1e-06) * gain_ref[...]).astype(BF16)
    raw = jnp.dot(normed, weight_ref[...], preferred_element_type=F32) + bias_ref[...]
    delta = jnp.maximum(raw, 0.0) + jnp.log1p(jnp.exp(-jnp.abs(raw)))
    columns = jnp.transpose(selected[:, rank_size:])
    rate = -jnp.exp(decay_ref[...])
    convolved = conv_ref[...]
    pushed = delta * convolved
    gate = (gate_ref[...].astype(F32) + gate_got_ref[...].astype(F32)).astype(BF16).astype(F32)
    gate = gate * jax.nn.sigmoid(gate)
    skipped = skip_ref[...] * convolved
    read = [None] * rows
    for r in range(reqs):
        state = state_ref[r]
        for t in range(rows // reqs):
            i = t * reqs + r
            bvec = columns[:states, i : i + 1]
            cvec = columns[states : 2 * states, i : i + 1]
            state = jnp.exp(delta[i : i + 1] * rate) * state + pushed[i : i + 1] * bvec
            read[i] = jnp.sum(state * cvec, axis=0, keepdims=True)
        state_out_ref[r] = state
    readout = jnp.concatenate(read, axis=0) + skipped
    gated_ref[...] = (readout * gate).astype(BF16)


def scan(got, gain, step, bias, decay, skip, conv, gate, gate_got, state):
    rows, channels = conv.shape
    return pl.pallas_call(
        scan_kernel,
        out_shape=(
            jax.ShapeDtypeStruct((rows, channels), BF16),
            jax.ShapeDtypeStruct(state.shape, F32),
        ),
        scratch_shapes=[pltpu.VMEM((gain.shape[0], channels), BF16)],
        compiler_params=pltpu.CompilerParams(vmem_limit_bytes=32 * 1024 * 1024),
        cost_estimate=pl.CostEstimate(
            flops=2 * rows * gain.shape[0] * channels + 8 * state.size,
            bytes_accessed=2 * gain.shape[0] * channels + 8 * state.size,
            transcendentals=4 * state.size,
        ),
        name="scan",
    )(got, gain[None], step, bias[None], decay, skip[None], conv, gate, gate_got, state)


def mix_kernel(where_ref, *refs):
    x_refs, w_refs, out_ref, total_ref = refs[:8], refs[8:12], refs[12], refs[13]
    rows = x_refs[0].shape[0]
    width = w_refs[0].shape[2]
    step = pl.program_id(0)

    @pl.when(step == 0)
    def _():
        total_ref[...] = jnp.zeros_like(total_ref)

    x = jnp.concatenate([x_ref[...] for x_ref in x_refs], axis=0)
    for i, w_ref in enumerate(w_refs):
        cols = slice(i * width, (i + 1) * width)
        total_ref[:, cols] += jnp.dot(x, w_ref[0], preferred_element_type=F32)

    @pl.when(step == pl.num_programs(0) - 1)
    def _():
        for j in range(8):
            row = pl.multiple_of(where_ref[4 + j] * rows, rows)
            for i in range(4):
                lane = pl.multiple_of(where_ref[i] * width, width)
                tile = total_ref[j * rows : (j + 1) * rows, i * width : (i + 1) * width]
                out_ref[pl.ds(row, rows), pl.ds(lane, width)] = tile.astype(BF16)


def mix(where, xs, near, far):
    rows, depth = xs[0].shape
    width = near.shape[2]
    tiles = 4
    tall = depth // tiles
    return pl.pallas_call(
        mix_kernel,
        grid=(tiles,),
        out_shape=jax.ShapeDtypeStruct((8 * rows, 4 * width), BF16),
        in_specs=[pl.BlockSpec(memory_space=pltpu.SMEM)]
        + [pl.BlockSpec((rows, tall), lambda i: (0, i))] * 8
        + [
            pl.BlockSpec((1, tall, width), lambda i: (0, i, 0)),
            pl.BlockSpec((1, tall, width), lambda i: (1, i, 0)),
        ]
        * 2,
        out_specs=pl.BlockSpec((8 * rows, 4 * width), lambda i: (0, 0)),
        scratch_shapes=[pltpu.VMEM((8 * rows, 4 * width), F32)],
        cost_estimate=pl.CostEstimate(
            flops=64 * rows * depth * width,
            bytes_accessed=8 * depth * width + 64 * rows * width,
            transcendentals=0,
        ),
        name="mix",
    )(where, *xs, near, near, far, far)


def local(
    token_ids,
    embed_table,
    norm_gain,
    in_weight,
    filter_weight,
    filter_bias,
    select_weight,
    step_gain,
    step_weight,
    step_bias,
    decay_log,
    skip_gain,
    out_weight,
    filter_state,
    scan_state,
):
    steps, reqs = token_ids.shape
    vocab_rows, width = embed_table.shape
    feats, _, channels = in_weight.shape
    rank_size = step_gain.shape[0]
    rows = steps * reqs
    nb, nc = count(BATCH), count(CHAN)
    tokens = nb * rows
    core = lax.axis_index("k")
    me = lax.axis_index(BATCH)
    features = norm_gain.shape[0]

    side = lax.axis_index("h")
    step_rows = in_order(step_weight, swap(step_weight, "h"), side, 0)
    step_rows = step_rows.reshape(2, -1, channels)
    step_rows = in_order(step_rows, swap(step_rows, "k"), core, 1).reshape(-1, channels)
    step_full = lax.all_gather(step_rows, "z", axis=0, tiled=True)
    in_flat = in_weight.reshape(feats, 2 * channels)

    ids = gather_copies(token_ids.reshape(rows), BATCH).reshape(nb // 2, 2, rows)
    ids = ids.transpose(1, 0, 2).reshape(tokens)
    ids, in_flat = lax.optimization_barrier((ids, in_flat))
    in_other = swap(in_flat, "k")
    out_pair = jnp.stack([out_weight, swap(out_weight, "k")])
    out_far = swap(out_pair, "h")
    vocab_index = me * vocab_rows + lax.broadcasted_iota(jnp.int32, (tokens, vocab_rows), 1)
    hot = (vocab_index == ids[:, None]).astype(BF16)
    picked = jnp.dot(hot, embed_table, preferred_element_type=F32).astype(BF16)
    picked = picked.reshape(2, nb // 2, rows, width)
    picked = add(take(picked, core), swap(take(picked, 1 - core), "k"))
    picked = lax.all_to_all(picked, ("h", "z"), 0, 0, tiled=True)
    own = jnp.sum(picked.astype(F32), axis=0).astype(BF16)
    embedded = gather_copies(own, CHAN).transpose(1, 0, 2).reshape(rows, features)
    embed_wide = embedded.astype(F32)
    mean_square = jnp.mean(embed_wide * embed_wide, axis=-1, keepdims=True)
    normed = (embed_wide * lax.rsqrt(mean_square + 1e-06) * norm_gain).astype(BF16)
    spread = normed.reshape(rows, nb // 2, 2 * feats).transpose(1, 0, 2)
    x = lax.all_to_all(spread, ("h", "z"), 0, 0, tiled=True).reshape(tokens // 2, 2 * feats)
    x_mine = lax.dynamic_slice_in_dim(x, core * feats, feats, axis=1)
    x_other = lax.dynamic_slice_in_dim(x, (1 - core) * feats, feats, axis=1)


    def project(which):
        cols = slice(which * channels, (which + 1) * channels)
        part = jnp.dot(x_mine, in_flat[:, cols], preferred_element_type=F32)
        part += jnp.dot(x_other, in_other[:, cols], preferred_element_type=F32)
        return part.astype(BF16).reshape(2, 8, rows, channels).transpose(1, 0, 2, 3)

    first, step_full = lax.optimization_barrier((project(0), step_full))
    sums = ring_sums([first, project(1)], "z")
    stream, stream_got, gate, gate_got = [
        piece
        for one in sums
        for piece in (take(one, side), swap(take(one, 1 - side), "h"))
    ]
    past = filter_state.transpose(1, 0, 2)
    convolved, past, part = convolve(
        stream, stream_got, past, filter_weight, filter_bias, select_weight.T, rank_size, nc
    )
    filter_out = past.transpose(1, 0, 2)
    got = lax.all_to_all(part, CHAN, 0, 0, tiled=True)
    step_blocks = step_full.reshape(8, 2, rank_size // 16, channels)
    gated, scan_now = scan(
        got, step_gain, step_blocks, step_bias, decay_log, skip_gain, convolved, gate, gate_got, scan_state
    )

    every = [gated] + [shift(gated, "z", -j) for j in range(1, 8)]
    place = jnp.arange(4, dtype=jnp.int32)
    place = (place // 2 + side) % 2 * 2 + (place + core) % 2
    turn = (jnp.arange(8, dtype=jnp.int32) + lax.axis_index("z")) % 8
    part_out = mix(jnp.concatenate([place, turn]), every, out_pair, out_far)
    per = rows // nc
    sent = part_out.reshape(8, nc, per, 4 * feats).transpose(1, 0, 2, 3)
    got = lax.all_to_all(sent, CHAN, 0, 0, tiled=True)
    mixed = jnp.sum(got.astype(F32), axis=0).astype(BF16).reshape(8, 1, per, 4 * feats)

    copies = jnp.broadcast_to(mixed, (8, nc, per, 4 * feats)).reshape(8 * nc, per, 4 * feats)
    home = lax.all_to_all(copies, ("z",) + CHAN, 0, 0, tiled=True)
    home = home.reshape(8, rows, 2, 2 * feats).transpose(1, 2, 0, 3).reshape(rows, features)
    home = lax.optimization_barrier(home)
    hidden = (embed_wide + home.astype(F32)).astype(BF16).reshape(steps, reqs, features)
    return (hidden, filter_out, scan_now)


def solution(mesh):
    fine = Mesh(mesh.devices.reshape([SIZES[axis] for axis in AXES]), AXES)
    return jax.shard_map(
        local,
        mesh=fine,
        in_specs=(
            P(None, BATCH),
            P(BATCH, CHAN),
            P(),
            P(BATCH, None, CHAN),
            P(None, CHAN),
            P(CHAN),
            P(CHAN, None),
            P(),
            P(BATCH, CHAN),
            P(CHAN),
            P(None, CHAN),
            P(CHAN),
            P(CHAN, BATCH),
            P(BATCH, None, CHAN),
            P(BATCH, None, CHAN),
        ),
        out_specs=(P(None, BATCH, None), P(BATCH, None, CHAN), P(BATCH, None, CHAN)),
        check_vma=False,
    )
```

```python
import jax
import jax.numpy as jnp
from jax import lax
from jax.experimental import pallas as pl
from jax.experimental.pallas import tpu as pltpu
from jax.sharding import Mesh, PartitionSpec as P

BATCH = ("h", "z", "k")
CHAN = ("x", "l")
SIZES = {"h": 2, "z": 8, "k": 2, "x": 4, "l": 2}
AXES = BATCH + CHAN
F32 = jnp.float32
BF16 = jnp.bfloat16


def count(axes):
    total = 1
    for axis in axes:
        total *= SIZES[axis]
    return total


def gather_copies(block, axes):
    copies = jnp.broadcast_to(block[None], (count(axes),) + block.shape)
    return lax.all_to_all(copies, axes, 0, 0, tiled=True)


def swap(block, axis):
    return lax.ppermute(block, axis, [(0, 1), (1, 0)])


def shift(block, axis, distance):
    n = SIZES[axis]
    return lax.ppermute(block, axis, [(i, (i + distance) % n) for i in range(n)])


def in_order(mine, other, index, axis):
    first = jnp.where(index == 0, mine, other)
    return jnp.concatenate([first, jnp.where(index == 0, other, mine)], axis=axis)


def take(block, index):
    return lax.dynamic_index_in_dim(block, index, keepdims=False)


def add(a, b):
    return (a.astype(F32) + b.astype(F32)).astype(BF16)


def ring_sums(parts, axis):
    n = SIZES[axis]
    here = lax.axis_index(axis)
    up = [None] * len(parts)
    down = [None] * len(parts)
    for away in range(n // 2, 0, -1):
        if up[0] is not None:
            up[0], down[0] = lax.optimization_barrier((up[0], down[0]))
        for i, part in enumerate(parts):
            term = take(part, (here + away) % n)
            up[i] = shift(term if up[i] is None else add(term, up[i]), axis, 1)
            if away < n // 2:
                term = take(part, (here - away) % n)
                down[i] = shift(term if down[i] is None else add(term, down[i]), axis, -1)
    return [
        (take(part, here).astype(F32) + u.astype(F32) + d.astype(F32)).astype(BF16)
        for part, u, d in zip(parts, up, down)
    ]


def convolve_kernel(mine_ref, got_ref, past_ref, taps_ref, bias_ref, select_ref, conv_ref, past_out_ref, part_ref):
    kept, reqs, _ = past_ref.shape
    rows = mine_ref.shape[0]
    steps = rows // reqs
    stream = (mine_ref[...].astype(F32) + got_ref[...].astype(F32)).astype(BF16).astype(F32)
    window = [past_ref[i] for i in range(kept)]
    window += [stream[i * reqs : (i + 1) * reqs] for i in range(steps)]
    for i in range(kept):
        past_out_ref[i] = window[steps + i]
    found = []
    for t in range(steps):
        total = window[t] * taps_ref[0:1, :]
        for i in range(1, kept + 1):
            total += window[t + i] * taps_ref[i : i + 1, :]
        total += bias_ref[...]
        found.append(total * jax.nn.sigmoid(total))
    convolved = jnp.concatenate(found, axis=0)
    conv_ref[...] = convolved
    low = convolved.astype(BF16)
    rank_size = part_ref.shape[2] - 128
    turned = (((1,), (1,)), ((), ()))
    rank = lax.dot_general(low, select_ref[:rank_size, :], turned, preferred_element_type=F32)
    rest = lax.dot_general(low, select_ref[rank_size:, :], turned, preferred_element_type=F32)
    rest = jnp.concatenate([rest, jnp.zeros((rows, 128 - rest.shape[1]), F32)], axis=1)
    for i in range(part_ref.shape[0]):
        part_ref[i, :, :rank_size] = rank
        part_ref[i, :, rank_size:] = rest


def convolve(mine, got, past, taps, bias, select, rank_size, copies):
    rows, channels = mine.shape
    width = rank_size + 128
    return pl.pallas_call(
        convolve_kernel,
        out_shape=(
            jax.ShapeDtypeStruct((rows, channels), F32),
            jax.ShapeDtypeStruct(past.shape, F32),
            jax.ShapeDtypeStruct((copies, rows, width), F32),
        ),
        compiler_params=pltpu.CompilerParams(vmem_limit_bytes=12 * 1024 * 1024),
        cost_estimate=pl.CostEstimate(
            flops=2 * rows * channels * width,
            bytes_accessed=2 * channels * width,
            transcendentals=rows * channels,
        ),
        name="convolve",
    )(mine, got, past, taps, bias[None], select)


def scan_kernel(
    got_ref, gain_ref, step_ref, bias_ref, decay_ref, skip_ref, conv_ref, gate_ref, gate_got_ref, state_ref,
    gated_ref, state_out_ref, weight_ref,
):
    reqs, states, _ = state_ref.shape
    rows = conv_ref.shape[0]
    rank_size = gain_ref.shape[1]
    turns, sides, tall, _ = step_ref.shape
    for z in range(turns):
        for h in range(sides):
            first = (h * turns + z) * tall
            weight_ref[first : first + tall, :] = step_ref[z, h]
    selected = got_ref[0]
    for i in range(1, got_ref.shape[0]):
        selected += got_ref[i]
    rank = selected[:, :rank_size]
    mean_square = jnp.mean(rank * rank, axis=-1, keepdims=True)
    normed = (rank * lax.rsqrt(mean_square + 1e-06) * gain_ref[...]).astype(BF16)
    raw = jnp.dot(normed, weight_ref[...], preferred_element_type=F32) + bias_ref[...]
    delta = jnp.maximum(raw, 0.0) + jnp.log1p(jnp.exp(-jnp.abs(raw)))
    columns = jnp.transpose(selected[:, rank_size:])
    rate = -jnp.exp(decay_ref[...])
    convolved = conv_ref[...]
    pushed = delta * convolved
    gate = (gate_ref[...].astype(F32) + gate_got_ref[...].astype(F32)).astype(BF16).astype(F32)
    gate = gate * jax.nn.sigmoid(gate)
    skipped = skip_ref[...] * convolved
    read = [None] * rows
    for r in range(reqs):
        state = state_ref[r]
        for t in range(rows // reqs):
            i = t * reqs + r
            bvec = columns[:states, i : i + 1]
            cvec = columns[states : 2 * states, i : i + 1]
            state = jnp.exp(delta[i : i + 1] * rate) * state + pushed[i : i + 1] * bvec
            read[i] = jnp.sum(state * cvec, axis=0, keepdims=True)
        state_out_ref[r] = state
    readout = jnp.concatenate(read, axis=0) + skipped
    gated_ref[...] = (readout * gate).astype(BF16)


def scan(got, gain, step, bias, decay, skip, conv, gate, gate_got, state):
    rows, channels = conv.shape
    return pl.pallas_call(
        scan_kernel,
        out_shape=(
            jax.ShapeDtypeStruct((rows, channels), BF16),
            jax.ShapeDtypeStruct(state.shape, F32),
        ),
        scratch_shapes=[pltpu.VMEM((gain.shape[0], channels), BF16)],
        compiler_params=pltpu.CompilerParams(vmem_limit_bytes=14 * 1024 * 1024),
        cost_estimate=pl.CostEstimate(
            flops=2 * rows * gain.shape[0] * channels + 8 * state.size,
            bytes_accessed=2 * gain.shape[0] * channels + 8 * state.size,
            transcendentals=4 * state.size,
        ),
        name="scan",
    )(got, gain[None], step, bias[None], decay, skip[None], conv, gate, gate_got, state)


def mix_kernel(where_ref, *refs):
    x_refs, near_ref, far_ref, out_ref = refs[:8], refs[8], refs[9], refs[10]
    rows = x_refs[0].shape[0]
    width = near_ref.shape[2]
    x = jnp.concatenate([x_ref[...] for x_ref in x_refs], axis=0)
    for i in range(4):
        w = near_ref[i] if i < 2 else far_ref[i - 2]
        total = jnp.dot(x, w, preferred_element_type=F32).astype(BF16)
        lane = pl.multiple_of(where_ref[i] * width, width)
        for j in range(8):
            row = pl.multiple_of(where_ref[4 + j] * rows, rows)
            out_ref[pl.ds(row, rows), pl.ds(lane, width)] = total[j * rows : (j + 1) * rows]


def mix(where, xs, near, far):
    rows, depth = xs[0].shape
    width = near.shape[2]
    return pl.pallas_call(
        mix_kernel,
        out_shape=jax.ShapeDtypeStruct((8 * rows, 4 * width), BF16),
        in_specs=[pl.BlockSpec(memory_space=pltpu.SMEM)]
        + [pl.BlockSpec(memory_space=pltpu.VMEM)] * 10,
        compiler_params=pltpu.CompilerParams(vmem_limit_bytes=12 * 1024 * 1024),
        cost_estimate=pl.CostEstimate(
            flops=64 * rows * depth * width,
            bytes_accessed=8 * depth * width + 64 * rows * width,
            transcendentals=0,
        ),
        name="mix",
    )(where, *xs, near, far)


def local(
    token_ids,
    embed_table,
    norm_gain,
    in_weight,
    filter_weight,
    filter_bias,
    select_weight,
    step_gain,
    step_weight,
    step_bias,
    decay_log,
    skip_gain,
    out_weight,
    filter_state,
    scan_state,
):
    steps, reqs = token_ids.shape
    vocab_rows, width = embed_table.shape
    feats, _, channels = in_weight.shape
    rank_size = step_gain.shape[0]
    rows = steps * reqs
    nb, nc = count(BATCH), count(CHAN)
    tokens = nb * rows
    core = lax.axis_index("k")
    me = lax.axis_index(BATCH)
    features = norm_gain.shape[0]

    side = lax.axis_index("h")
    step_rows = in_order(step_weight, swap(step_weight, "h"), side, 0)
    step_rows = step_rows.reshape(2, -1, channels)
    step_rows = in_order(step_rows, swap(step_rows, "k"), core, 1).reshape(-1, channels)
    step_full = lax.all_gather(step_rows, "z", axis=0, tiled=True)
    in_flat = in_weight.reshape(feats, 2 * channels)

    ids = gather_copies(token_ids.reshape(rows), BATCH).reshape(nb // 2, 2, rows)
    ids = ids.transpose(1, 0, 2).reshape(tokens)
    ids, in_flat = lax.optimization_barrier((ids, in_flat))
    in_other = swap(in_flat, "k")
    out_pair = jnp.stack([out_weight, swap(out_weight, "k")])
    out_far = swap(out_pair, "h")
    vocab_index = me * vocab_rows + lax.broadcasted_iota(jnp.int32, (tokens, vocab_rows), 1)
    hot = (vocab_index == ids[:, None]).astype(BF16)
    picked = jnp.dot(hot, embed_table, preferred_element_type=F32).astype(BF16)
    picked = picked.reshape(2, nb // 2, rows, width)
    picked = add(take(picked, core), swap(take(picked, 1 - core), "k"))
    picked = lax.all_to_all(picked, ("h", "z"), 0, 0, tiled=True)
    own = jnp.sum(picked.astype(F32), axis=0).astype(BF16)
    embedded = gather_copies(own, CHAN).transpose(1, 0, 2).reshape(rows, features)
    embed_wide = embedded.astype(F32)
    mean_square = jnp.mean(embed_wide * embed_wide, axis=-1, keepdims=True)
    normed = (embed_wide * lax.rsqrt(mean_square + 1e-06) * norm_gain).astype(BF16)
    spread = normed.reshape(rows, nb // 2, 2 * feats).transpose(1, 0, 2)
    x = lax.all_to_all(spread, ("h", "z"), 0, 0, tiled=True).reshape(tokens // 2, 2 * feats)
    x_mine = lax.dynamic_slice_in_dim(x, core * feats, feats, axis=1)
    x_other = lax.dynamic_slice_in_dim(x, (1 - core) * feats, feats, axis=1)


    def project(which):
        cols = slice(which * channels, (which + 1) * channels)
        part = jnp.dot(x_mine, in_flat[:, cols], preferred_element_type=F32)
        part += jnp.dot(x_other, in_other[:, cols], preferred_element_type=F32)
        return part.astype(BF16).reshape(2, 8, rows, channels).transpose(1, 0, 2, 3)

    first, step_full = lax.optimization_barrier((project(0), step_full))
    sums = ring_sums([first, project(1)], "z")
    stream, stream_got, gate, gate_got = [
        piece
        for one in sums
        for piece in (take(one, side), swap(take(one, 1 - side), "h"))
    ]
    past = filter_state.transpose(1, 0, 2)
    convolved, past, part = convolve(
        stream, stream_got, past, filter_weight, filter_bias, select_weight.T, rank_size, nc
    )
    filter_out = past.transpose(1, 0, 2)
    got = lax.all_to_all(part, CHAN, 0, 0, tiled=True)
    step_blocks = step_full.reshape(8, 2, rank_size // 16, channels)
    gated, scan_now = scan(
        got, step_gain, step_blocks, step_bias, decay_log, skip_gain, convolved, gate, gate_got, scan_state
    )

    every = [gated] + [shift(gated, "z", -j) for j in range(1, 8)]
    place = jnp.arange(4, dtype=jnp.int32)
    place = (place // 2 + side) % 2 * 2 + (place + core) % 2
    turn = (jnp.arange(8, dtype=jnp.int32) + lax.axis_index("z")) % 8
    part_out = mix(jnp.concatenate([place, turn]), every, out_pair, out_far)
    per = rows // nc
    sent = part_out.reshape(8, nc, per, 4 * feats).transpose(1, 0, 2, 3)
    got = lax.all_to_all(sent, CHAN, 0, 0, tiled=True)
    mixed = jnp.sum(got.astype(F32), axis=0).astype(BF16).reshape(8, 1, per, 4 * feats)

    copies = jnp.broadcast_to(mixed, (8, nc, per, 4 * feats)).reshape(8 * nc, per, 4 * feats)
    home = lax.all_to_all(copies, ("z",) + CHAN, 0, 0, tiled=True)
    home = home.reshape(8, rows, 2, 2 * feats).transpose(1, 2, 0, 3).reshape(rows, features)
    home = lax.optimization_barrier(home)
    hidden = (embed_wide + home.astype(F32)).astype(BF16).reshape(steps, reqs, features)
    return (hidden, filter_out, scan_now)


def solution(mesh):
    fine = Mesh(mesh.devices.reshape([SIZES[axis] for axis in AXES]), AXES)
    return jax.shard_map(
        local,
        mesh=fine,
        in_specs=(
            P(None, BATCH),
            P(BATCH, CHAN),
            P(),
            P(BATCH, None, CHAN),
            P(None, CHAN),
            P(CHAN),
            P(CHAN, None),
            P(),
            P(BATCH, CHAN),
            P(CHAN),
            P(None, CHAN),
            P(CHAN),
            P(CHAN, BATCH),
            P(BATCH, None, CHAN),
            P(BATCH, None, CHAN),
        ),
        out_specs=(P(None, BATCH, None), P(BATCH, None, CHAN), P(BATCH, None, CHAN)),
        check_vma=False,
    )
```
